256 devices in a mesh: row: 16 (over z, x_hi), col: 16 (over x_lo, y, core).
Axes of the slice: x: 4 (x_hi: 2, x_lo: 2; x = x_hi * 2 + x_lo), y: 4, z: 8, core: 2. Of those that a mesh axis runs over, the one named last changes fastest.
Arguments:
- sensitivity: bfloat16 [16, 16, 8, 96, 256], P('row', 'col'), may hold values from -0.41992188 to 0.41992188
- block_ids: int32 [16, 16, 8], replicated, may hold values from 0 to 63, as said below
- covariance: float32 [64, 256], replicated, may hold values from 0.05 to 1
Outputs:
- gram: float32 [16, 1536, 16, 1536], P('row', None, 'col')
The draws below stay inside these ranges and needn't reach their ends.
Inputs may be any that keep to these rules, and one draw needn't show every extreme that they name: `block_ids`: the 8 ids of one station group at one period are distinct; footprints widen with the period index.
All inputs are finite; a program needn't handle non-finite values.
Results may differ from the reference program's by a relative error of at most 0.0024.
Values may be sent and summed in bfloat16 or wider, within the bound.
A program may use at most 128 MiB of HBM per device.

```python
import math
import jax
import jax.numpy as jnp
from jax import lax

SEG = 96
K = 8
BS = 256
NB = 64
N_ROW = 16
N_COL = 16


def draw_block_ids(key, part):
    key = jax.random.fold_in(key, 11)
    scores = jax.random.randint(key, (N_ROW, N_COL, NB), 0, 1 << 20)
    offsets = jnp.arange(NB, dtype=jnp.int32)
    period = jnp.arange(N_COL, dtype=jnp.int32)
    span = 2 * K + period * (NB - 2 * K) // max(N_COL - 1, 1)
    outside = offsets[None, :] >= span[:, None]
    ends = (offsets[None, :] == 0) | (offsets[None, :] == span[:, None] - 1)
    keyed = scores * NB + offsets[None, None, :]
    keyed = jnp.where(outside[None, :, :], (1 << 30) + offsets[None, None, :], keyed)
    keyed = jnp.where(ends[None, :, :], offsets[None, None, :] - NB, keyed)
    order = jnp.argsort(keyed, axis=-1, stable=True)[..., :K].astype(jnp.int32)
    center = jnp.arange(N_ROW, dtype=jnp.int32) * NB // N_ROW
    return ((center[:, None, None] + order) % NB).astype(jnp.int32)


def block_levels(stream_key, shape, shards, low, top_value):
    gain = 1.0
    for position, parts in shards:
        heights = jax.random.uniform(jax.random.fold_in(jax.random.fold_in(stream_key, 6), position), (parts,), jnp.float32, low / len(shards), top_value / len(shards))
        gain = gain * jnp.repeat(jnp.exp(heights), shape[position] // parts).reshape((-1,) + (1,) * (len(shape) - 1 - position))
    return gain


def gaussian(key, extent, spread, reach, cuts=(), kind=jnp.bfloat16):
    values = spread * jax.random.normal(key, extent, jnp.float32)
    if cuts:
        values = values * block_levels(key, extent, cuts, -0.22, 0.18)
    return jnp.clip(values, -reach, reach).astype(kind)


def setup_inputs(seed: int = 0) -> dict:
    keys = jax.random.split(jax.random.key(seed), 4)
    sensitivity = gaussian(keys[0], (N_ROW, N_COL, K, SEG, BS), 0.07, 0.41992188, ((0, 16), (1, 16)))
    block_ids = draw_block_ids(jax.random.fold_in(keys[3], 71), 0)
    covariance = jnp.clip(jnp.exp(jax.random.uniform(keys[2], (NB, BS), jnp.float32, math.log(0.05), math.log(1.0))), 0.05, 1.0)
    return dict(sensitivity=sensitivity, block_ids=block_ids, covariance=covariance)


def tile_columns(rows, row_ids, cols, col_ids):
    cols_wide = cols.astype(jnp.float32)

    def one_row(args):
        block, ids = args
        match = (ids[None, :, None] == col_ids[:, None, :]).astype(jnp.float32)
        aligned = jnp.einsum('akl,alje->akje', match, cols_wide)
        return jnp.einsum('kie,akje->iaj', block.astype(jnp.float32), aligned)

    result = lax.map(one_row, (rows, row_ids))
    return result.reshape(rows.shape[0] * rows.shape[2], cols.shape[0] * cols.shape[2])


def reference(sensitivity, block_ids, covariance):
    factors = covariance[block_ids]
    scaled = (sensitivity.astype(jnp.float32) * factors[:, :, :, None, :]).astype(jnp.bfloat16)

    def one_tile(index):
        row_index = index // N_COL
        col_index = index % N_COL
        rows = lax.dynamic_index_in_dim(scaled, row_index, 0, keepdims=False)
        row_ids = lax.dynamic_index_in_dim(block_ids, row_index, 0, keepdims=False)
        cols = lax.dynamic_index_in_dim(sensitivity, col_index, 1, keepdims=False)
        col_ids = lax.dynamic_index_in_dim(block_ids, col_index, 1, keepdims=False)
        return tile_columns(rows, row_ids, cols, col_ids)

    tiles = lax.map(one_tile, jnp.arange(N_ROW * N_COL, dtype=jnp.int32))
    tiles = tiles.reshape(N_ROW, N_COL, N_COL * SEG, N_ROW * SEG)
    return jnp.transpose(tiles, (0, 2, 1, 3))
```

```python
import functools
import jax
import jax.numpy as jnp
from jax import lax
from jax.experimental import pallas as pl
from jax.experimental.pallas import tpu as pltpu
from jax.sharding import PartitionSpec as P

MESH = pl.DeviceIdType.MESH
NX, NY, NZ = 4, 4, 8


def gather_kernel(chunk, ids_ref, sens_ref, cov_ref, cols_ref, rows_ref, own, scaled, local_sem, send_sem, recv_sem):
    row = lax.axis_index("row")
    col = lax.axis_index("col")
    z, x_hi = row // 2, row % 2
    x_lo, y, core = col // 8, (col // 2) % 4, col % 2
    blocks = sens_ref.shape[0]
    half = blocks // 2

    def station(z_at, x_hi_at):
        return ((z_at + NZ) % NZ) * 2 + x_hi_at

    def period(x_lo_at, y_at, core_at):
        return (x_lo_at * NY + (y_at + NY) % NY) * 2 + core_at

    z_dev = {d: (station(z + d, x_hi), col) for d in (1, -1)}
    y_dev = {d: (row, period(x_lo, y + d, core)) for d in (1, -1)}
    far_dev = (station(z, 1 - x_hi), col)
    side_dev = (row, period(1 - x_lo, y, core))
    twin_dev = (row, period(x_lo, y, 1 - core))

    load = pltpu.make_async_copy(sens_ref, own, local_sem.at[0])
    load.start()
    keep = pltpu.make_async_copy(sens_ref, cols_ref.at[row], local_sem.at[1])
    keep.start()

    barrier = pltpu.get_barrier_semaphore()
    partners = [z_dev[1], z_dev[-1], y_dev[1], y_dev[-1], far_dev, side_dev, twin_dev]
    for device in partners:
        pl.semaphore_signal(barrier, inc=1, device_id=device, device_id_type=MESH)
    pl.semaphore_wait(barrier, len(partners))

    copies = {}

    def send(key, src, dst, device):
        n = len(copies)
        copy = pltpu.make_async_remote_copy(
            src_ref=src, dst_ref=dst, send_sem=send_sem.at[n], recv_sem=recv_sem.at[n], device_id=device, device_id_type=MESH
        )
        copy.start()
        copies[key] = copy

    def z_blocks(name, d, step):
        first, size = streams[name]
        if step == 4:
            return (first, size // 2) if d == 1 else (first + size // 2, size // 2)
        return first, size

    streams = {}
    names = {"b": [], "a": [], "p": []}
    for kind, base in (("b", half), ("a", 0), ("p", 0)):
        for first in range(base, base + half, chunk):
            streams[(kind, first)] = (first, chunk)
            names[kind].append((kind, first))

    def send_z(name, d, step):
        first, size = z_blocks(name, d, step)
        slot = station(z - d * (step - 1), 1 - x_hi if name[0] == "p" else x_hi)
        src = sens_ref if (step == 1 and name[0] != "p") else cols_ref.at[slot]
        send(("z", name, d, step), src.at[pl.ds(first, size)], cols_ref.at[slot, pl.ds(first, size)], z_dev[d])

    def send_far(name, d, step):
        first, size = z_blocks(name, d, step)
        slot = station(z - d * step, x_hi)
        src = sens_ref if step == 0 else cols_ref.at[slot]
        send(("far", name, d, step), src.at[pl.ds(first, size)], cols_ref.at[slot, pl.ds(first, size)], far_dev)

    def take_z(name, d, step):
        copies[("z", name, d, step)].wait_recv()
        if step < 4:
            send_z(name, d, step + 1)
        if name[0] == "b":
            send_far(name, d, step)

    for name in names["b"]:
        for d in (1, -1):
            send_z(name, d, 1)
    for name in names["b"]:
        send_far(name, 1, 0)
    for name in names["a"]:
        for d in (1, -1):
            send_z(name, d, 1)

    load.wait()
    for k in range(blocks):
        factor = cov_ref[pl.ds(ids_ref[(row * 16 + col) * blocks + k], 1), :]
        scaled[k] = (own[k].astype(jnp.float32) * factor).astype(jnp.bfloat16)
    keep_row = pltpu.make_async_copy(scaled, rows_ref.at[col], local_sem.at[2])
    keep_row.start()
    send(("side",), scaled, rows_ref.at[col], side_dev)
    for d in (1, -1):
        send(("y", 0, d), scaled, rows_ref.at[col], y_dev[d])
    send(("twin", "own"), scaled, rows_ref.at[col], twin_dev)
    for name in names["a"]:
        send_far(name, 1, 0)

    def twin(key, slot, first, size):
        ref = rows_ref.at[slot, pl.ds(first, size)]
        send(("twin", key), ref, ref, twin_dev)

    def take_y(line, d):
        copies[("y", line, d)].wait_recv()
        slot = period(x_lo if line == 0 else 1 - x_lo, y - d, core)
        first = 0 if d == 1 else half
        ref = rows_ref.at[slot, pl.ds(first, half)]
        send(("y2", line, d), ref, ref, y_dev[d])
        twin(("y", line, d), slot, 0, blocks)

    def take_y2(line, d):
        copies[("y2", line, d)].wait_recv()
        slot = period(x_lo if line == 0 else 1 - x_lo, y - 2 * d, core)
        twin(("y2", line, d), slot, 0 if d == 1 else half, half)

    def z_round(kinds, step):
        for kind in kinds:
            for name in names[kind]:
                for d in (1, -1):
                    take_z(name, d, step)

    z_round("b", 1)
    for d in (1, -1):
        take_y(0, d)
    z_round("a", 1)
    copies[("side",)].wait_recv()
    slot = period(1 - x_lo, y, core)
    for d in (1, -1):
        send(("y", 1, d), rows_ref.at[slot], rows_ref.at[slot], y_dev[d])
    twin("side", slot, 0, blocks)
    z_round("b", 2)
    for name in names["a"]:
        copies[("far", name, 1, 0)].wait_recv()
        for d in (1, -1):
            send_z(("p", name[1]), d, 1)
    z_round("a", 2)
    for d in (1, -1):
        take_y2(0, d)
    z_round("p", 1)
    z_round("b", 3)
    for d in (1, -1):
        take_y(1, d)
    z_round("a", 3)
    z_round("p", 2)
    z_round("b", 4)
    for d in (1, -1):
        take_y2(1, d)
    z_round("a", 4)
    z_round("p", 3)
    z_round("p", 4)

    taken = {("side",)}
    for key, copy in copies.items():
        copy.wait_send()
        if key[0] == "twin" or (key[0] == "far" and key[1][0] == "b"):
            copy.wait_recv()
    keep.wait()
    keep_row.wait()


def gather(ids, sens, cov, chunk=4):
    blocks, seg, cells = sens.shape
    out = jax.ShapeDtypeStruct((16, blocks, seg, cells), sens.dtype)
    copies = 200
    return pl.pallas_call(
        functools.partial(gather_kernel, chunk),
        out_shape=(out, out),
        in_specs=[
            pl.BlockSpec(memory_space=pltpu.SMEM),
            pl.BlockSpec(memory_space=pl.ANY),
            pl.BlockSpec(memory_space=pltpu.VMEM),
        ],
        out_specs=(pl.BlockSpec(memory_space=pl.ANY), pl.BlockSpec(memory_space=pl.ANY)),
        scratch_shapes=[
            pltpu.VMEM((blocks, seg, cells), sens.dtype),
            pltpu.VMEM((blocks, seg, cells), sens.dtype),
            pltpu.SemaphoreType.DMA((3,)),
            pltpu.SemaphoreType.DMA((copies,)),
            pltpu.SemaphoreType.DMA((copies,)),
        ],
        compiler_params=pltpu.CompilerParams(collective_id=1, has_side_effects=True),
        name="gather",
    )(ids, sens, cov)


NT = (((1,), (1,)), ((), ()))
WIDE = 16
NARROW = 4
GROUP = 4


def product_kernel(ids_ref, cols_hbm, rows_hbm, out_hbm, cols, rows, total, stage, count, entry, pairs, starts, in_sem, out_sem):
    row = lax.axis_index("row")
    col = lax.axis_index("col")
    stations, blocks, seg, cells = cols_hbm.shape
    groups = stations // GROUP
    per = GROUP * blocks
    model = count.shape[0]

    def load(hbm, held, n, sem):
        return pltpu.make_async_copy(hbm.at[pl.ds(n * GROUP, GROUP)], held.at[pl.ds(n * GROUP, GROUP)], in_sem.at[sem])

    for n in range(groups):
        load(cols_hbm, cols, n, n).start()
    for n in range(groups):
        load(rows_hbm, rows, n, groups + n).start()

    rows[stations] = jnp.zeros(rows.shape[1:], rows.dtype)
    total[...] = jnp.zeros_like(total)

    @pl.loop(0, model)
    def _(n):
        count[n] = 0

    @pl.loop(0, stations * blocks)
    def _(e):
        n = ids_ref[((e // blocks) * stations + col) * blocks + e % blocks]
        c = count[n]
        entry[n * stations + c] = e
        count[n] = c + 1

    def fill(g, at):
        starts[g] = at

        def one(e, at):
            n = ids_ref[row * stations * blocks + e]
            c = count[n]

            def put(i, _):
                pairs[at + i] = e * 256 + entry[n * stations + i]
                return 0

            lax.fori_loop(0, c, put, 0)
            return at + c

        at = lax.fori_loop(g * per, (g + 1) * per, one, at)
        padded = ((at + NARROW - 1) // NARROW) * NARROW

        def pad(i, _):
            pairs[i] = stations * blocks * 256
            return 0

        lax.fori_loop(at, padded, pad, 0)
        return padded

    end = lax.fori_loop(0, groups, fill, 0)
    starts[groups] = end

    def multiply(at, width):
        found = [pairs[at + i] for i in range(width)]
        left = [p // 256 for p in found]
        right = [p % 256 for p in found]
        results = [
            lax.dot_general(
                rows[e // blocks, e % blocks], cols[f // blocks, f % blocks], NT, preferred_element_type=jnp.float32
            )
            for e, f in zip(left, right)
        ]
        for e, f, r in zip(left, right, results):
            total[(e // blocks) * stations + f // blocks, :, :seg] += r

    lane = lax.broadcasted_iota(jnp.int32, (seg, 128), 1)
    for n in range(groups):
        load(cols_hbm, cols, n, n).wait()
    writes = []
    for g in range(groups):
        load(rows_hbm, rows, g, groups + g).wait()
        first = starts[g]
        size = starts[g + 1] - first
        wide = size // WIDE

        @pl.loop(0, wide)
        def _(t):
            multiply(first + t * WIDE, WIDE)

        @pl.loop(0, (size - wide * WIDE) // NARROW)
        def _(t):
            multiply(first + wide * WIDE + t * NARROW, NARROW)

        @pl.loop(g * GROUP, (g + 1) * GROUP)
        def _(b):
            for q in range(stations // 4):
                part = [total[b * stations + q * 4 + p] for p in range(4)]
                r1, r2, r3 = [pltpu.roll(part[p], 128 - 32 * p, axis=1) for p in (1, 2, 3)]
                tiles = [
                    jnp.where(lane < 96, part[0], r1),
                    jnp.where(lane < 64, r1, r2),
                    jnp.where(lane < 32, r2, r3),
                ]
                for t in range(3):
                    stage[pl.ds(b * seg * 12 + q * 3 + t, seg, stride=12), :] = tiles[t]

        chunk = GROUP * seg * 12
        write = pltpu.make_async_copy(
            stage.at[pl.ds(g * chunk, chunk)], out_hbm.at[pl.ds(g * chunk, chunk)], out_sem.at[g]
        )
        write.start()
        writes.append(write)
    for write in writes:
        write.wait()


def product(ids, cols, rows):
    stations, blocks, seg, cells = cols.shape
    lines = stations * seg * stations * seg // 128
    return pl.pallas_call(
        product_kernel,
        out_shape=jax.ShapeDtypeStruct((lines, 128), jnp.float32),
        in_specs=[
            pl.BlockSpec(memory_space=pltpu.SMEM),
            pl.BlockSpec(memory_space=pl.ANY),
            pl.BlockSpec(memory_space=pl.ANY),
        ],
        out_specs=pl.BlockSpec(memory_space=pl.ANY),
        scratch_shapes=[
            pltpu.VMEM((stations, blocks, seg, cells), cols.dtype),
            pltpu.VMEM((stations + 1, blocks, seg, cells), cols.dtype),
            pltpu.VMEM((stations * (stations + 1), seg, 128), jnp.float32),
            pltpu.VMEM((lines, 128), jnp.float32),
            pltpu.SMEM((64,), jnp.int32),
            pltpu.SMEM((64 * stations,), jnp.int32),
            pltpu.SMEM((stations * stations * blocks + 64,), jnp.int32),
            pltpu.SMEM((8,), jnp.int32),
            pltpu.SemaphoreType.DMA((8,)),
            pltpu.SemaphoreType.DMA((4,)),
        ],
        compiler_params=pltpu.CompilerParams(vmem_limit_bytes=48 * 2**20),
        name="product",
    )(ids, cols, rows)


def body(sensitivity, block_ids, covariance):
    ids = block_ids.reshape(-1)
    cols, rows = gather(ids, sensitivity[0, 0], covariance)
    lines = product(ids, cols, rows)
    stations, _, seg, _ = cols.shape
    return lines.reshape(1, stations * seg, 1, stations * seg)


def solution(mesh):
    placed = (P("row", "col", None, None, None), P(), P())
    return jax.shard_map(
        body, mesh=mesh, in_specs=placed, out_specs=P("row", None, "col", None), check_vma=False
    )
```

```python
import functools

import jax
import jax.numpy as jnp
from jax import lax
from jax.experimental import pallas as pl
from jax.experimental.pallas import tpu as pltpu
from jax.sharding import PartitionSpec as P

MESH = pl.DeviceIdType.MESH
NT = (((1,), (1,)), ((), ()))
NY, NZ = 4, 8
SLOTS = 4
BATCH = 16


def place():
    row = lax.axis_index("row")
    col = lax.axis_index("col")
    return row, col, row // 2, row % 2, col // 8, (col // 2) % 4, col % 2


def station(z, x_hi):
    return ((z + NZ) % NZ) * 2 + x_hi


def period(x_lo, y, core):
    return (x_lo * NY + (y + NY) % NY) * 2 + core


def row_order():
    _, _, _, _, x_lo, y, core = place()
    return [period(x, y + d, c) for x in (x_lo, 1 - x_lo) for c in (core, 1 - core) for d in (0, -1, 1, 2)]


def col_order():
    _, _, z, x_hi, _, _, _ = place()
    far = 1 - x_hi
    steps = [(0, x_hi), (-1, x_hi), (1, x_hi), (0, far), (-2, x_hi), (2, x_hi), (-1, far), (1, far)]
    steps += [(-3, x_hi), (3, x_hi), (-2, far), (2, far), (4, x_hi), (-3, far), (3, far), (4, far)]
    return [station(z + d, x) for d, x in steps]


def gather_kernel(
    ids_ref, sens_ref, cov_ref, total_hbm, cols_hbm, rows_hbm, more_ref,
    total, cols, rows, held_cols, held_rows, own, scaled, table, slots, col_at, row_at, local_sem, send_sem, recv_sem,
):
    row, col, z, x_hi, x_lo, y, core = place()
    blocks, seg, cells = sens_ref.shape
    half = blocks // 2

    z_dev = {d: (station(z + d, x_hi), col) for d in (1, -1)}
    y_dev = {d: (row, period(x_lo, y + d, core)) for d in (1, -1)}
    far_dev = (station(z, 1 - x_hi), col)
    side_dev = (row, period(1 - x_lo, y, core))
    twin_dev = (row, period(x_lo, y, 1 - core))

    load = pltpu.make_async_copy(sens_ref, own, local_sem.at[0])
    load.start()

    barrier = pltpu.get_barrier_semaphore()
    partners = [z_dev[1], z_dev[-1], y_dev[1], y_dev[-1], far_dev, side_dev, twin_dev]
    for device in partners:
        pl.semaphore_signal(barrier, inc=1, device_id=device, device_id_type=MESH)
    pl.semaphore_wait(barrier, len(partners))

    copies = {}

    def send(key, src, dst, device):
        n = len(copies)
        copy = pltpu.make_async_remote_copy(
            src_ref=src, dst_ref=dst, send_sem=send_sem.at[n], recv_sem=recv_sem.at[n], device_id=device, device_id_type=MESH
        )
        copy.start()
        copies[key] = copy

    def taken(*key):
        copies[key].wait_recv()

    def piece(kind, d, step):
        first = half if kind == "b" else 0
        if step < 4:
            return pl.ds(first, half), pl.ds(0, seg)
        return pl.ds(first, half), pl.ds(0 if d == 1 else seg // 2, seg // 2)

    def send_z(kind, d, step):
        part = piece(kind, d, step)
        slot = station(z - d * (step - 1), 1 - x_hi if kind == "p" else x_hi)
        src = sens_ref if (step == 1 and kind != "p") else cols.at[slot]
        send(("z", kind, d, step), src.at[part], cols.at[(slot, *part)], z_dev[d])

    def send_far(kind, d, step):
        part = piece(kind, d, step)
        slot = station(z - d * step, x_hi)
        src = sens_ref if step == 0 else cols.at[slot]
        send(("far", kind, d, step), src.at[part], cols.at[(slot, *part)], far_dev)

    def take_z(kind, step):
        for d in (1, -1):
            taken("z", kind, d, step)
            if step < 4:
                send_z(kind, d, step + 1)
            if kind == "b":
                send_far(kind, d, step)

    for kind in "ba":
        for d in (1, -1):
            send_z(kind, d, 1)

    load.wait()
    lane = lax.broadcasted_iota(jnp.int32, (1, 16), 1)
    model = lax.broadcasted_iota(jnp.int32, (cov_ref.shape[0], 1), 0)
    for k in range(blocks):
        mine = jnp.sum(jnp.where(lane == col, ids_ref[row, k : k + 1, :], 0), axis=1, keepdims=True)
        factor = jnp.sum(jnp.where(model == mine, cov_ref[...], 0.0), axis=0, keepdims=True)
        scaled[k] = (own[k].astype(jnp.float32) * factor).astype(jnp.bfloat16)
    send(("side",), scaled, rows.at[col], side_dev)
    for d in (1, -1):
        send(("y", 0, d), scaled, rows.at[col], y_dev[d])
    send(("twin", 0, 0), scaled, rows.at[col], twin_dev)
    send_far("a", 1, 0)
    send_far("b", 1, 0)

    def twin(line, shift, slot, first, size):
        ref = rows.at[slot, pl.ds(first, size)]
        send(("twin", line, shift), ref, ref, twin_dev)

    def take_y(line):
        for d in (1, -1):
            taken("y", line, d)
            slot = period(x_lo if line == 0 else 1 - x_lo, y - d, core)
            ref = rows.at[slot, pl.ds(0 if d == 1 else half, half)]
            send(("y2", line, d), ref, ref, y_dev[d])
            twin(line, d, slot, 0, blocks)

    def take_y2(line):
        for d in (1, -1):
            taken("y2", line, d)
            slot = period(x_lo if line == 0 else 1 - x_lo, y - 2 * d, core)
            twin(line, 2 * d, slot, 0 if d == 1 else half, half)

    def take_twin(line):
        for shift in (0, 1, -1, 2, -2):
            taken("twin", line, shift)

    at_col = lax.broadcasted_iota(jnp.int32, (16, 16), 0)
    at_row = lax.broadcasted_iota(jnp.int32, (16, 16), 1)
    other = jnp.logical_or(at_col != row, at_row != col)
    left = [jnp.broadcast_to(ids_ref[row, k : k + 1, :], (16, 16)) for k in range(blocks)]
    right = [
        jnp.broadcast_to(jnp.sum(jnp.where(at_row == col, ids_ref[:, l, :], 0), axis=1, keepdims=True), (16, 16))
        for l in range(blocks)
    ]
    count = jnp.zeros((16, 16), jnp.int32)
    found = [jnp.full((16, 16), blocks * 16, jnp.int32) for _ in range(blocks)]
    for k in range(blocks):
        for l in range(blocks):
            hit = jnp.logical_and(left[k] == right[l], other)
            for s in range(min(blocks, k + 1)):
                found[s] = jnp.where(jnp.logical_and(hit, count == s), k * 16 + l, found[s])
            count = count + hit.astype(jnp.int32)
    table[...] = jnp.zeros_like(table)
    more_ref[...] = jnp.zeros_like(more_ref)
    for s in range(SLOTS):
        table[s, :, 0:16] = found[s]
    for s in range(SLOTS, blocks):
        more_ref[s - SLOTS, :, 0:16] = found[s]
    more_ref[blocks - SLOTS, :, 0:16] = count
    more_ref[blocks - SLOTS + 1, 0:1, 0:16] = jnp.max(count, axis=0, keepdims=True)
    fill = pltpu.make_async_copy(table, slots, local_sem.at[1])
    fill.start()
    fill.wait()
    for n, (a, b) in enumerate(zip(col_order(), row_order())):
        col_at[n] = a
        row_at[n] = b

    kept = []

    def keep(src, dst):
        copy = pltpu.make_async_copy(src, dst, local_sem.at[2 + len(kept)])
        copy.start()
        kept.append(copy)

    def hold_col(n):
        slot = col_order()[n]
        src = own if n == 0 else cols.at[slot]
        keep(src, cols_hbm.at[slot])
        for k in range(blocks):
            held_cols[n * blocks + k] = src[k]

    def hold_row(n):
        slot = row_order()[n]
        src = scaled if n == 0 else rows.at[slot]
        keep(src, rows_hbm.at[slot])
        for k in range(blocks):
            held_rows[n * (blocks + 1) + k] = src[k]
        held_rows[n * (blocks + 1) + blocks] = jnp.zeros((seg, cells), jnp.bfloat16)

    def multiply(half_rows, first, last):
        @pl.loop(first, last)
        def _(n):
            a = col_at[n]
            results = []
            for m in range(8 * half_rows, 8 * half_rows + 8):
                b = row_at[m]
                codes = [slots[s, a, b] for s in range(SLOTS)]
                lhs = jnp.concatenate([held_rows[m * (blocks + 1) + (c >> 4)] for c in codes], axis=1)
                rhs = jnp.concatenate([held_cols[n * blocks + (c & 15)] for c in codes], axis=1)
                results.append(lax.dot_general(lhs, rhs, NT, preferred_element_type=jnp.float32))
            for m, result in enumerate(results):
                total[n, 8 * half_rows + m, :, 0:seg] = result

        if half_rows == 0 and first == 0:
            lhs = jnp.concatenate([scaled[k] for k in range(blocks)], axis=1)
            rhs = jnp.concatenate([own[k] for k in range(blocks)], axis=1)
            total[0, 0, :, 0:seg] = lax.dot_general(lhs, rhs, NT, preferred_element_type=jnp.float32)
        part = pl.ds(first, last - first), pl.ds(8 * half_rows, 8)
        keep(total.at[part], total_hbm.at[part])

    def take_far(step):
        for d in (1, -1):
            taken("far", "b", d, step)

    def hold_cols(*which):
        for n in which:
            hold_col(n)

    hold_row(0)
    hold_col(0)
    take_z("b", 1)
    take_y(0)
    take_z("a", 1)
    taken("side")
    slot = period(1 - x_lo, y, core)
    for d in (1, -1):
        send(("y", 1, d), rows.at[slot], rows.at[slot], y_dev[d])
    twin(1, 0, slot, 0, blocks)
    hold_cols(1, 2)
    take_z("b", 2)
    taken("far", "a", 1, 0)
    for d in (1, -1):
        send_z("p", d, 1)
    take_z("a", 2)
    take_y2(0)
    hold_cols(4, 5)
    taken("far", "b", 1, 0)
    hold_cols(3)
    for n in (1, 2, 3):
        hold_row(n)
    take_z("p", 1)
    take_twin(0)
    for n in range(4, 8):
        hold_row(n)
    multiply(0, 0, 3)
    take_z("b", 3)
    multiply(0, 3, 6)
    take_y(1)
    take_z("a", 3)
    take_far(1)
    hold_cols(6, 7)
    multiply(0, 6, 8)
    take_z("p", 2)
    take_y2(1)
    hold_cols(8, 9)
    multiply(0, 8, 10)
    take_z("b", 4)
    take_far(2)
    hold_cols(10, 11)
    multiply(0, 10, 12)
    take_twin(1)
    for n in range(8, 16):
        hold_row(n)
    multiply(1, 0, 4)
    take_z("a", 4)
    multiply(1, 4, 8)
    take_z("p", 3)
    multiply(1, 8, 12)
    hold_cols(12)
    take_far(3)
    hold_cols(13, 14)
    multiply(0, 12, 15)
    multiply(1, 12, 15)
    take_z("p", 4)
    take_far(4)
    hold_cols(15)
    multiply(0, 15, 16)
    multiply(1, 15, 16)

    for copy in copies.values():
        copy.wait_send()
    for copy in kept:
        copy.wait()


def gather(ids, sens, cov):
    blocks, seg, cells = sens.shape
    shard = (16, blocks, seg, cells)
    out = jax.ShapeDtypeStruct(shard, sens.dtype)
    copies = 64
    vmem = pl.BlockSpec(memory_space=pltpu.VMEM)
    hbm = pl.BlockSpec(memory_space=pl.ANY)
    return pl.pallas_call(
        gather_kernel,
        out_shape=(
            jax.ShapeDtypeStruct((16, 16, seg, 128), jnp.float32),
            out,
            out,
            jax.ShapeDtypeStruct((blocks - SLOTS + 2, 16, 128), jnp.int32),
        ),
        in_specs=[vmem, hbm, vmem],
        out_specs=(hbm, hbm, hbm, vmem),
        scratch_shapes=[
            pltpu.VMEM((16, 16, seg, 128), jnp.float32),
            pltpu.VMEM(shard, sens.dtype),
            pltpu.VMEM(shard, sens.dtype),
            pltpu.VMEM((16 * blocks, seg, cells), sens.dtype),
            pltpu.VMEM((16 * (blocks + 1), seg, cells), sens.dtype),
            pltpu.VMEM((blocks, seg, cells), sens.dtype),
            pltpu.VMEM((blocks, seg, cells), sens.dtype),
            pltpu.VMEM((SLOTS, 16, 128), jnp.int32),
            pltpu.SMEM((SLOTS, 16, 128), jnp.int32),
            pltpu.SMEM((16,), jnp.int32),
            pltpu.SMEM((16,), jnp.int32),
            pltpu.SemaphoreType.DMA((2 + 48,)),
            pltpu.SemaphoreType.DMA((copies,)),
            pltpu.SemaphoreType.DMA((copies,)),
        ],
        compiler_params=pltpu.CompilerParams(collective_id=1, has_side_effects=True, vmem_limit_bytes=60 * 2**20),
        name="gather",
    )(ids, sens, cov)


def product_kernel(
    total_hbm, more_hbm, cols_hbm, rows_hbm, out_hbm,
    total, stage, more, row_of, col_of, entry, left, right, more_sem, in_sem, left_sem, right_sem, out_sem,
):
    blocks, seg = cols_hbm.shape[1:3]
    tiles = 12
    fetch = pltpu.make_async_copy(more_hbm, more, more_sem.at[0])
    fetch.start()
    for n, (a, b) in enumerate(zip(col_order(), row_order())):
        col_of[a] = n
        row_of[b] = n

    def read(b):
        return pltpu.make_async_copy(total_hbm.at[:, row_of[b]], total.at[b], in_sem.at[b])

    @pl.loop(0, 16)
    def _(b):
        read(b).start()

    fetch.wait()

    def late(b):
        return more[blocks - SLOTS + 1, 0, b] > SLOTS

    def scan_row(b, n):
        def scan(a, n):
            def put(s, n):
                entry[n] = (b * 16 + a) * 256 + more[s, a, b]
                return n + 1

            return lax.fori_loop(0, jnp.maximum(more[blocks - SLOTS, a, b] - SLOTS, 0), put, n)

        return lax.fori_loop(0, jnp.where(late(b), 16, 0), scan, n)

    n_more = lax.fori_loop(0, 16, scan_row, 0)

    def blocks_of(e, i):
        code = entry[e]
        a, b, k, l = (code >> 8) & 15, code >> 12, (code >> 4) & 15, code & 15
        return (
            a,
            b,
            pltpu.make_async_copy(rows_hbm.at[b, k], left.at[i], left_sem.at[i]),
            pltpu.make_async_copy(cols_hbm.at[a, l], right.at[i], right_sem.at[i]),
        )

    def start_batch(first):
        @pl.loop(0, jnp.minimum(n_more - first, BATCH))
        def _(i):
            _, _, lhs, rhs = blocks_of(first + i, i)
            lhs.start()
            rhs.start()

    def write(b):
        chunk = seg * tiles
        part = pl.ds(pl.multiple_of(b * chunk, chunk), chunk)
        return pltpu.make_async_copy(stage.at[part], out_hbm.at[part], out_sem.at[b])

    start_batch(0)
    lane = lax.broadcasted_iota(jnp.int32, (seg, 128), 1)

    @pl.loop(0, 16)
    def _(b):
        read(b).wait()
        for q in range(4):
            part = [total[b, col_of[q * 4 + p]] for p in range(4)]
            r1, r2, r3 = [pltpu.roll(part[p], 128 - 32 * p, axis=1) for p in (1, 2, 3)]
            joined = [
                jnp.where(lane < 96, part[0], r1),
                jnp.where(lane < 64, r1, r2),
                jnp.where(lane < 32, r2, r3),
            ]
            for t in range(3):
                stage[pl.ds(b * seg * tiles + q * 3 + t, seg, stride=tiles), :] = joined[t]

        @pl.when(jnp.logical_not(late(b)))
        def _():
            write(b).start()

    @pl.when(n_more > 0)
    def _():
        @pl.loop(0, (n_more + BATCH - 1) // BATCH)
        def _(batch):
            first = batch * BATCH

            @pl.when(batch > 0)
            def _():
                start_batch(first)

            @pl.loop(0, jnp.minimum(n_more - first, BATCH))
            def _(i):
                a, b, lhs, rhs = blocks_of(first + i, i)
                lhs.wait()
                rhs.wait()
                r = lax.dot_general(left[i], right[i], NT, preferred_element_type=jnp.float32)
                r = jnp.concatenate([r, jnp.zeros((seg, 128 - seg), jnp.float32)], axis=1)
                t = a * seg // 128
                shift = a * seg % 128
                r = pltpu.roll(r, shift, axis=1)
                base = b * seg * tiles
                here = pl.ds(base + t, seg, stride=tiles)
                stage[here, :] = stage[here, :] + jnp.where(lane >= shift, r, 0.0)
                there = pl.ds(base + jnp.minimum(t + 1, tiles - 1), seg, stride=tiles)
                stage[there, :] = stage[there, :] + jnp.where(lane < shift, r, 0.0)

        @pl.loop(0, 16)
        def _(b):
            @pl.when(late(b))
            def _():
                write(b).start()

    @pl.loop(0, 16)
    def _(b):
        write(b).wait()


def product(total, more, cols, rows):
    stations, blocks, seg, cells = cols.shape
    lines = stations * seg * stations * seg // 128
    hbm = pl.BlockSpec(memory_space=pl.ANY)
    return pl.pallas_call(
        product_kernel,
        out_shape=jax.ShapeDtypeStruct((lines, 128), jnp.float32),
        in_specs=[hbm, hbm, hbm, hbm],
        out_specs=hbm,
        scratch_shapes=[
            pltpu.VMEM(total.shape, jnp.float32),
            pltpu.VMEM((lines, 128), jnp.float32),
            pltpu.SMEM(more.shape, jnp.int32),
            pltpu.SMEM((16,), jnp.int32),
            pltpu.SMEM((16,), jnp.int32),
            pltpu.SMEM((stations * stations * blocks,), jnp.int32),
            pltpu.VMEM((BATCH, seg, cells), cols.dtype),
            pltpu.VMEM((BATCH, seg, cells), cols.dtype),
            pltpu.SemaphoreType.DMA((1,)),
            pltpu.SemaphoreType.DMA((16,)),
            pltpu.SemaphoreType.DMA((BATCH,)),
            pltpu.SemaphoreType.DMA((BATCH,)),
            pltpu.SemaphoreType.DMA((16,)),
        ],
        compiler_params=pltpu.CompilerParams(vmem_limit_bytes=60 * 2**20),
        name="product",
    )(total, more, cols, rows)


def body(sensitivity, block_ids, covariance):
    ids = jnp.transpose(block_ids, (0, 2, 1))
    total, cols, rows, more = gather(ids, sensitivity[0, 0], covariance)
    lines = product(total, more, cols, rows)
    stations, _, seg, _ = cols.shape
    return lines.reshape(1, stations * seg, 1, stations * seg)


def solution(mesh):
    placed = (P("row", "col", None, None, None), P(), P())
    return jax.shard_map(
        body, mesh=mesh, in_specs=placed, out_specs=P("row", None, "col", None), check_vma=False
    )
```

```python
import functools

import jax
import jax.numpy as jnp
from jax import lax
from jax.experimental import pallas as pl
from jax.experimental.pallas import tpu as pltpu
from jax.sharding import PartitionSpec as P

MESH = pl.DeviceIdType.MESH
NT = (((1,), (1,)), ((), ()))
NY, NZ = 4, 8
SLOTS = 4
BATCH = 16


def place():
    row = lax.axis_index("row")
    col = lax.axis_index("col")
    return row, col, row // 2, row % 2, col // 8, (col // 2) % 4, col % 2


def station(z, x_hi):
    return ((z + NZ) % NZ) * 2 + x_hi


def period(x_lo, y, core):
    return (x_lo * NY + (y + NY) % NY) * 2 + core


def row_order():
    _, _, _, _, x_lo, y, core = place()
    return [period(x, y + d, c) for x in (x_lo, 1 - x_lo) for c in (core, 1 - core) for d in (0, -1, 1, 2)]


def col_order():
    _, _, z, x_hi, _, _, _ = place()
    far = 1 - x_hi
    steps = [(0, x_hi), (-1, x_hi), (1, x_hi), (0, far), (-2, x_hi), (2, x_hi), (-1, far), (1, far)]
    steps += [(-3, x_hi), (3, x_hi), (-2, far), (2, far), (4, x_hi), (-3, far), (3, far), (4, far)]
    return [station(z + d, x) for d, x in steps]


def gather_kernel(
    ids_ref, sens_ref, cov_ref, total, cols_hbm, rows_hbm, more_hbm,
    cols, rows, held_cols, held_rows, own, scaled, table, more, slots, col_at, row_at, local_sem, send_sem, recv_sem,
):
    row, col, z, x_hi, x_lo, y, core = place()
    blocks, seg, cells = sens_ref.shape
    half = blocks // 2

    z_dev = {d: (station(z + d, x_hi), col) for d in (1, -1)}
    y_dev = {d: (row, period(x_lo, y + d, core)) for d in (1, -1)}
    far_dev = (station(z, 1 - x_hi), col)
    side_dev = (row, period(1 - x_lo, y, core))
    twin_dev = (row, period(x_lo, y, 1 - core))

    load = pltpu.make_async_copy(sens_ref, own, local_sem.at[0])
    load.start()

    barrier = pltpu.get_barrier_semaphore()
    partners = [z_dev[1], z_dev[-1], y_dev[1], y_dev[-1], far_dev, side_dev, twin_dev]
    for device in partners:
        pl.semaphore_signal(barrier, inc=1, device_id=device, device_id_type=MESH)
    pl.semaphore_wait(barrier, len(partners))

    copies = {}

    def send(key, src, dst, device):
        n = len(copies)
        copy = pltpu.make_async_remote_copy(
            src_ref=src, dst_ref=dst, send_sem=send_sem.at[n], recv_sem=recv_sem.at[n], device_id=device, device_id_type=MESH
        )
        copy.start()
        copies[key] = copy

    def taken(*key):
        copies[key].wait_recv()

    def piece(kind, d, step):
        first = half if kind == "b" else 0
        if step < 4:
            return pl.ds(first, half), pl.ds(0, seg)
        return pl.ds(first, half), pl.ds(0 if d == 1 else seg // 2, seg // 2)

    def send_z(kind, d, step):
        part = piece(kind, d, step)
        slot = station(z - d * (step - 1), 1 - x_hi if kind == "p" else x_hi)
        src = sens_ref if (step == 1 and kind != "p") else cols.at[slot]
        send(("z", kind, d, step), src.at[part], cols.at[(slot, *part)], z_dev[d])

    def send_far(kind, d, step):
        part = piece(kind, d, step)
        slot = station(z - d * step, x_hi)
        src = sens_ref if step == 0 else cols.at[slot]
        send(("far", kind, d, step), src.at[part], cols.at[(slot, *part)], far_dev)

    def take_z(kind, step):
        for d in (1, -1):
            taken("z", kind, d, step)
            if step < 4:
                send_z(kind, d, step + 1)
            if kind == "b":
                send_far(kind, d, step)

    for kind in "ba":
        for d in (1, -1):
            send_z(kind, d, 1)

    load.wait()
    lane = lax.broadcasted_iota(jnp.int32, (1, 16), 1)
    model = lax.broadcasted_iota(jnp.int32, (cov_ref.shape[0], 1), 0)
    for k in range(blocks):
        mine = jnp.sum(jnp.where(lane == col, ids_ref[row, k : k + 1, :], 0), axis=1, keepdims=True)
        factor = jnp.sum(jnp.where(model == mine, cov_ref[...], 0.0), axis=0, keepdims=True)
        scaled[k] = (own[k].astype(jnp.float32) * factor).astype(jnp.bfloat16)
    send(("side",), scaled, rows.at[col], side_dev)
    for d in (1, -1):
        send(("y", 0, d), scaled, rows.at[col], y_dev[d])
    send(("twin", 0, 0), scaled, rows.at[col], twin_dev)
    send_far("a", 1, 0)
    send_far("b", 1, 0)

    def twin(line, shift, slot, first, size):
        ref = rows.at[slot, pl.ds(first, size)]
        send(("twin", line, shift), ref, ref, twin_dev)

    def take_y(line):
        for d in (1, -1):
            taken("y", line, d)
            slot = period(x_lo if line == 0 else 1 - x_lo, y - d, core)
            ref = rows.at[slot, pl.ds(0 if d == 1 else half, half)]
            send(("y2", line, d), ref, ref, y_dev[d])
            twin(line, d, slot, 0, blocks)

    def take_y2(line):
        for d in (1, -1):
            taken("y2", line, d)
            slot = period(x_lo if line == 0 else 1 - x_lo, y - 2 * d, core)
            twin(line, 2 * d, slot, 0 if d == 1 else half, half)

    def take_twin(line):
        for shift in (0, 1, -1, 2, -2):
            taken("twin", line, shift)

    at_col = lax.broadcasted_iota(jnp.int32, (16, 16), 0)
    at_row = lax.broadcasted_iota(jnp.int32, (16, 16), 1)
    left = [jnp.broadcast_to(ids_ref[row, k : k + 1, :], (16, 16)) for k in range(blocks)]
    right = [
        jnp.broadcast_to(jnp.sum(jnp.where(at_row == col, ids_ref[:, l, :], 0), axis=1, keepdims=True), (16, 16))
        for l in range(blocks)
    ]
    count = jnp.zeros((16, 16), jnp.int32)
    found = [jnp.full((16, 16), blocks * 16, jnp.int32) for _ in range(blocks)]
    for k in range(blocks):
        for l in range(blocks):
            hit = left[k] == right[l]
            for s in range(min(blocks, k + 1)):
                found[s] = jnp.where(jnp.logical_and(hit, count == s), k * 16 + l, found[s])
            count = count + hit.astype(jnp.int32)
    table[...] = jnp.zeros_like(table)
    more[...] = jnp.zeros_like(more)
    for s in range(blocks):
        table[s, :, 0:16] = found[s]
    for s in range(SLOTS, blocks):
        more[s - SLOTS, :, 0:16] = found[s]
    count = jnp.where(at_col == row, 0, count)
    more[blocks - SLOTS, :, 0:16] = count
    more[blocks - SLOTS + 1, 0:1, 0:16] = jnp.max(count, axis=0, keepdims=True)
    fill = pltpu.make_async_copy(table, slots, local_sem.at[1])
    fill.start()
    fill.wait()
    for n, (a, b) in enumerate(zip(col_order(), row_order())):
        col_at[n] = a
        row_at[n] = b

    kept = []

    def keep(src, dst):
        copy = pltpu.make_async_copy(src, dst, local_sem.at[2 + len(kept)])
        copy.start()
        kept.append(copy)

    def hold_col(n):
        slot = col_order()[n]
        src = own if n == 0 else cols.at[slot]
        keep(src, cols_hbm.at[slot])
        for k in range(blocks):
            held_cols[n * blocks + k] = src[k]

    def hold_row(n):
        slot = row_order()[n]
        src = scaled if n == 0 else rows.at[slot]
        keep(src, rows_hbm.at[slot])
        for k in range(blocks):
            held_rows[n * (blocks + 1) + k] = src[k]
        held_rows[n * (blocks + 1) + blocks] = jnp.zeros((seg, cells), jnp.bfloat16)

    def multiply(half_rows, first, last, width=SLOTS):
        @pl.loop(first, last)
        def _(n):
            a = col_at[n]
            results = []
            for m in range(8 * half_rows, 8 * half_rows + 8):
                b = row_at[m]
                codes = [slots[s, a, b] for s in range(width)]
                lhs = jnp.concatenate([held_rows[m * (blocks + 1) + (c >> 4)] for c in codes], axis=1)
                rhs = jnp.concatenate([held_cols[n * blocks + (c & 15)] for c in codes], axis=1)
                results.append(lax.dot_general(lhs, rhs, NT, preferred_element_type=jnp.float32))
            for m, result in enumerate(results):
                total[n, 8 * half_rows + m, :, 0:seg] = result

    def take_far(step):
        for d in (1, -1):
            taken("far", "b", d, step)

    def hold_cols(*which):
        for n in which:
            hold_col(n)

    hold_row(0)
    hold_col(0)
    keep(more, more_hbm)
    take_z("b", 1)
    take_y(0)
    take_z("a", 1)
    taken("side")
    slot = period(1 - x_lo, y, core)
    for d in (1, -1):
        send(("y", 1, d), rows.at[slot], rows.at[slot], y_dev[d])
    twin(1, 0, slot, 0, blocks)
    hold_cols(1, 2)
    take_z("b", 2)
    taken("far", "a", 1, 0)
    for d in (1, -1):
        send_z("p", d, 1)
    take_z("a", 2)
    take_y2(0)
    hold_cols(4, 5)
    taken("far", "b", 1, 0)
    hold_cols(3)
    for n in (1, 2, 3):
        hold_row(n)
    take_z("p", 1)
    take_twin(0)
    for n in range(4, 8):
        hold_row(n)
    multiply(0, 0, 1, blocks)
    multiply(0, 1, 3)
    take_z("b", 3)
    multiply(0, 3, 6)
    take_y(1)
    take_z("a", 3)
    take_far(1)
    hold_cols(6, 7)
    multiply(0, 6, 8)
    take_z("p", 2)
    take_y2(1)
    hold_cols(8, 9)
    multiply(0, 8, 10)
    take_z("b", 4)
    take_far(2)
    hold_cols(10, 11)
    multiply(0, 10, 12)
    take_twin(1)
    for n in range(8, 16):
        hold_row(n)
    multiply(1, 0, 1, blocks)
    multiply(1, 1, 4)
    take_z("a", 4)
    multiply(1, 4, 8)
    take_z("p", 3)
    multiply(1, 8, 12)
    hold_cols(12)
    take_far(3)
    hold_cols(13, 14)
    multiply(0, 12, 15)
    multiply(1, 12, 15)
    take_z("p", 4)
    take_far(4)
    hold_cols(15)
    multiply(0, 15, 16)
    multiply(1, 15, 16)

    for copy in copies.values():
        copy.wait_send()
    for copy in kept:
        copy.wait()


def gather(ids, sens, cov):
    blocks, seg, cells = sens.shape
    shard = (16, blocks, seg, cells)
    copies = 64
    vmem = pl.BlockSpec(memory_space=pltpu.VMEM)
    hbm = pl.BlockSpec(memory_space=pl.ANY)
    return pl.pallas_call(
        gather_kernel,
        out_shape=(
            pltpu.VMEM((16, 16, seg, 128), jnp.float32),
            pltpu.HBM(shard, sens.dtype),
            pltpu.HBM(shard, sens.dtype),
            pltpu.HBM((blocks - SLOTS + 2, 16, 128), jnp.int32),
        ),
        in_specs=[vmem, hbm, vmem],
        out_specs=(vmem, hbm, hbm, hbm),
        scratch_shapes=[
            pltpu.VMEM(shard, sens.dtype),
            pltpu.VMEM(shard, sens.dtype),
            pltpu.VMEM((16 * blocks, seg, cells), sens.dtype),
            pltpu.VMEM((16 * (blocks + 1), seg, cells), sens.dtype),
            pltpu.VMEM((blocks, seg, cells), sens.dtype),
            pltpu.VMEM((blocks, seg, cells), sens.dtype),
            pltpu.VMEM((blocks, 16, 128), jnp.int32),
            pltpu.VMEM((blocks - SLOTS + 2, 16, 128), jnp.int32),
            pltpu.SMEM((blocks, 16, 128), jnp.int32),
            pltpu.SMEM((16,), jnp.int32),
            pltpu.SMEM((16,), jnp.int32),
            pltpu.SemaphoreType.DMA((2 + 48,)),
            pltpu.SemaphoreType.DMA((copies,)),
            pltpu.SemaphoreType.DMA((copies,)),
        ],
        compiler_params=pltpu.CompilerParams(collective_id=1, has_side_effects=True, vmem_limit_bytes=40 * 2**20),
        name="gather",
    )(ids, sens, cov)


def product_kernel(
    total, more_hbm, cols_hbm, rows_hbm, out_hbm,
    stage, more, row_of, col_of, entry, first_of, left, right, more_sem, left_sem, right_sem, out_sem,
):
    blocks, seg = cols_hbm.shape[1:3]
    tiles = 12
    fetch = pltpu.make_async_copy(more_hbm, more, more_sem.at[0])
    fetch.start()
    for n, (a, b) in enumerate(zip(col_order(), row_order())):
        col_of[a] = n
        row_of[b] = n
    lane = lax.broadcasted_iota(jnp.int32, (seg, 128), 1)

    def join(b):
        m = row_of[b]
        for q in range(4):
            part = [total[col_of[q * 4 + p], m] for p in range(4)]
            r1, r2, r3 = [pltpu.roll(part[p], 128 - 32 * p, axis=1) for p in (1, 2, 3)]
            joined = [
                jnp.where(lane < 96, part[0], r1),
                jnp.where(lane < 64, r1, r2),
                jnp.where(lane < 32, r2, r3),
            ]
            for t in range(3):
                stage[pl.ds(b * seg * tiles + q * 3 + t, seg, stride=tiles), :] = joined[t]

    def write(b):
        chunk = seg * tiles
        part = pl.ds(pl.multiple_of(b * chunk, chunk), chunk)
        return pltpu.make_async_copy(stage.at[part], out_hbm.at[part], out_sem.at[b])

    def late(b):
        return more[blocks - SLOTS + 1, 0, b] > SLOTS

    def scan_row(b, n):
        first_of[b] = n

        def scan(a, n):
            def put(s, n):
                entry[n] = (b * 16 + a) * 256 + more[s, a, b]
                return n + 1

            return lax.fori_loop(0, jnp.maximum(more[blocks - SLOTS, a, b] - SLOTS, 0), put, n)

        return lax.fori_loop(0, jnp.where(late(b), 16, 0), scan, n)

    def blocks_of(e):
        code = entry[e]
        i = e % BATCH
        a, b, k, l = (code >> 8) & 15, code >> 12, (code >> 4) & 15, code & 15
        return (
            a,
            pltpu.make_async_copy(rows_hbm.at[b, k], left.at[i], left_sem.at[i]),
            pltpu.make_async_copy(cols_hbm.at[a, l], right.at[i], right_sem.at[i]),
        )

    def start(e):
        _, lhs, rhs = blocks_of(e)
        lhs.start()
        rhs.start()

    def add(b):
        @pl.loop(first_of[b], first_of[b + 1])
        def _(e):
            @pl.when(e >= BATCH)
            def _():
                start(e)

            a, lhs, rhs = blocks_of(e)
            lhs.wait()
            rhs.wait()
            i = e % BATCH
            r = lax.dot_general(left[i], right[i], NT, preferred_element_type=jnp.float32)
            r = jnp.concatenate([r, jnp.zeros((seg, 128 - seg), jnp.float32)], axis=1)
            t = a * seg // 128
            shift = a * seg % 128
            r = pltpu.roll(r, shift, axis=1)
            base = b * seg * tiles
            here = pl.ds(base + t, seg, stride=tiles)
            stage[here, :] = stage[here, :] + jnp.where(lane >= shift, r, 0.0)
            there = pl.ds(base + jnp.minimum(t + 1, tiles - 1), seg, stride=tiles)
            stage[there, :] = stage[there, :] + jnp.where(lane < shift, r, 0.0)

    pl.loop(0, 4)(join)
    fetch.wait()
    n_more = lax.fori_loop(0, 16, scan_row, 0)
    first_of[16] = n_more
    pl.loop(0, jnp.minimum(n_more, BATCH))(start)

    @pl.loop(0, 4)
    def _(b):
        @pl.when(jnp.logical_not(late(b)))
        def _():
            write(b).start()

    @pl.loop(4, 10)
    def _(b):
        join(b)

        @pl.when(jnp.logical_not(late(b)))
        def _():
            write(b).start()

    @pl.loop(0, 16)
    def _(b):
        @pl.when(late(b))
        def _():
            @pl.when(b >= 10)
            def _():
                join(b)

            add(b)
            write(b).start()

    @pl.loop(10, 16)
    def _(b):
        @pl.when(jnp.logical_not(late(b)))
        def _():
            join(b)
            write(b).start()

    @pl.loop(0, 16)
    def _(b):
        write(b).wait()


def product(total, more, cols, rows):
    stations, blocks, seg, cells = cols.shape
    lines = stations * seg * stations * seg // 128
    hbm = pl.BlockSpec(memory_space=pl.ANY)
    return pl.pallas_call(
        product_kernel,
        out_shape=jax.ShapeDtypeStruct((lines, 128), jnp.float32),
        in_specs=[pl.BlockSpec(memory_space=pltpu.VMEM), hbm, hbm, hbm],
        out_specs=hbm,
        scratch_shapes=[
            pltpu.VMEM((lines, 128), jnp.float32),
            pltpu.SMEM(more.shape, jnp.int32),
            pltpu.SMEM((16,), jnp.int32),
            pltpu.SMEM((16,), jnp.int32),
            pltpu.SMEM((stations * stations * blocks,), jnp.int32),
            pltpu.SMEM((stations + 1,), jnp.int32),
            pltpu.VMEM((BATCH, seg, cells), cols.dtype),
            pltpu.VMEM((BATCH, seg, cells), cols.dtype),
            pltpu.SemaphoreType.DMA((1,)),
            pltpu.SemaphoreType.DMA((BATCH,)),
            pltpu.SemaphoreType.DMA((BATCH,)),
            pltpu.SemaphoreType.DMA((16,)),
        ],
        compiler_params=pltpu.CompilerParams(vmem_limit_bytes=14 * 2**20),
        name="product",
    )(total, more, cols, rows)


def body(sensitivity, block_ids, covariance):
    def in_hbm(x):
        return pltpu.with_memory_space_constraint(x, pltpu.HBM)

    ids = jnp.transpose(block_ids, (0, 2, 1))
    total, cols, rows, more = gather(in_hbm(ids), in_hbm(sensitivity[0, 0]), in_hbm(covariance))
    total = pltpu.with_memory_space_constraint(total, pltpu.VMEM)
    more, cols, rows = in_hbm(more), in_hbm(cols), in_hbm(rows)
    lines = product(total, more, cols, rows)
    stations, _, seg, _ = cols.shape
    return lines.reshape(1, stations * seg, 1, stations * seg)


def solution(mesh):
    placed = (P("row", "col", None, None, None), P(), P())
    return jax.shard_map(
        body, mesh=mesh, in_specs=placed, out_specs=P("row", None, "col", None), check_vma=False
    )
```

```python
import functools

import jax
import jax.numpy as jnp
from jax import lax
from jax.experimental import pallas as pl
from jax.experimental.pallas import tpu as pltpu
from jax.sharding import PartitionSpec as P

MESH = pl.DeviceIdType.MESH
NT = (((1,), (1,)), ((), ()))
NY, NZ = 4, 8
SLOTS = 4
BATCH = 16


def place():
    row = lax.axis_index("row")
    col = lax.axis_index("col")
    return row, col, row // 2, row % 2, col // 8, (col // 2) % 4, col % 2


def station(z, x_hi):
    return ((z + NZ) % NZ) * 2 + x_hi


def period(x_lo, y, core):
    return (x_lo * NY + (y + NY) % NY) * 2 + core


def row_order():
    _, _, _, _, x_lo, y, core = place()
    return [period(x, y + d, c) for x in (x_lo, 1 - x_lo) for c in (core, 1 - core) for d in (0, -1, 1, 2)]


def col_order():
    _, _, z, x_hi, _, _, _ = place()
    far = 1 - x_hi
    steps = [(0, x_hi), (-1, x_hi), (1, x_hi), (0, far), (-2, x_hi), (2, x_hi), (-1, far), (1, far)]
    steps += [(-3, x_hi), (3, x_hi), (-2, far), (2, far), (4, x_hi), (-3, far), (3, far), (4, far)]
    return [station(z + d, x) for d, x in steps]


def gather_kernel(
    ids_hbm, sens_ref, cov_hbm, total, cols_hbm, rows_hbm, more_hbm,
    ids_ref, cov_ref, cols, rows, held_cols, held_rows, own, scaled, table, more, slots, col_at, row_at, local_sem, send_sem, recv_sem,
):
    row, col, z, x_hi, x_lo, y, core = place()
    blocks, seg, cells = sens_ref.shape
    half = blocks // 2

    z_dev = {d: (station(z + d, x_hi), col) for d in (1, -1)}
    y_dev = {d: (row, period(x_lo, y + d, core)) for d in (1, -1)}
    far_dev = (station(z, 1 - x_hi), col)
    side_dev = (row, period(1 - x_lo, y, core))
    twin_dev = (row, period(x_lo, y, 1 - core))

    barrier = pltpu.get_barrier_semaphore()
    partners = [z_dev[1], z_dev[-1], y_dev[1], y_dev[-1], far_dev, side_dev, twin_dev]
    for device in partners:
        pl.semaphore_signal(barrier, inc=1, device_id=device, device_id_type=MESH)
    loads = [
        pltpu.make_async_copy(src, dst, local_sem.at[n])
        for n, (src, dst) in enumerate([(sens_ref, own), (ids_hbm, ids_ref), (cov_hbm, cov_ref)])
    ]
    for load in loads:
        load.start()
    pl.semaphore_wait(barrier, len(partners))

    copies = {}

    def send(key, src, dst, device):
        n = len(copies)
        copy = pltpu.make_async_remote_copy(
            src_ref=src, dst_ref=dst, send_sem=send_sem.at[n], recv_sem=recv_sem.at[n], device_id=device, device_id_type=MESH
        )
        copy.start()
        copies[key] = copy

    def taken(*key):
        copies[key].wait_recv()

    def piece(kind, d, step):
        first = half if kind == "b" else 0
        if step < 4:
            return pl.ds(first, half), pl.ds(0, seg)
        return pl.ds(first, half), pl.ds(0 if d == 1 else seg // 2, seg // 2)

    def send_z(kind, d, step):
        part = piece(kind, d, step)
        slot = station(z - d * (step - 1), 1 - x_hi if kind == "p" else x_hi)
        src = sens_ref if (step == 1 and kind != "p") else cols.at[slot]
        send(("z", kind, d, step), src.at[part], cols.at[(slot, *part)], z_dev[d])

    def send_far(kind, d, step):
        part = piece(kind, d, step)
        slot = station(z - d * step, x_hi)
        src = sens_ref if step == 0 else cols.at[slot]
        send(("far", kind, d, step), src.at[part], cols.at[(slot, *part)], far_dev)

    def take_z(kind, step):
        for d in (1, -1):
            taken("z", kind, d, step)
            if step < 4:
                send_z(kind, d, step + 1)
            if kind == "b":
                send_far(kind, d, step)

    for kind in "ba":
        for d in (1, -1):
            send_z(kind, d, 1)

    for load in loads:
        load.wait()
    lane = lax.broadcasted_iota(jnp.int32, (1, 16), 1)
    model = lax.broadcasted_iota(jnp.int32, (cov_ref.shape[0], 1), 0)
    for k in range(blocks):
        mine = jnp.sum(jnp.where(lane == col, ids_ref[row, k : k + 1, :], 0), axis=1, keepdims=True)
        factor = jnp.sum(jnp.where(model == mine, cov_ref[...], 0.0), axis=0, keepdims=True)
        scaled[k] = (own[k].astype(jnp.float32) * factor).astype(jnp.bfloat16)
    send(("side",), scaled, rows.at[col], side_dev)
    for d in (1, -1):
        send(("y", 0, d), scaled, rows.at[col], y_dev[d])
    send(("twin", 0, 0), scaled, rows.at[col], twin_dev)
    send_far("a", 1, 0)
    send_far("b", 1, 0)

    def twin(line, shift, slot, first, size):
        ref = rows.at[slot, pl.ds(first, size)]
        send(("twin", line, shift), ref, ref, twin_dev)

    def take_y(line):
        for d in (1, -1):
            taken("y", line, d)
            slot = period(x_lo if line == 0 else 1 - x_lo, y - d, core)
            ref = rows.at[slot, pl.ds(0 if d == 1 else half, half)]
            send(("y2", line, d), ref, ref, y_dev[d])
            twin(line, d, slot, 0, blocks)

    def take_y2(line):
        for d in (1, -1):
            taken("y2", line, d)
            slot = period(x_lo if line == 0 else 1 - x_lo, y - 2 * d, core)
            twin(line, 2 * d, slot, 0 if d == 1 else half, half)

    def take_twin(line):
        for shift in (0, 1, -1, 2, -2):
            taken("twin", line, shift)

    at_col = lax.broadcasted_iota(jnp.int32, (16, 16), 0)
    at_row = lax.broadcasted_iota(jnp.int32, (16, 16), 1)
    left = [jnp.broadcast_to(ids_ref[row, k : k + 1, :], (16, 16)) for k in range(blocks)]
    right = [
        jnp.broadcast_to(jnp.sum(jnp.where(at_row == col, ids_ref[:, l, :], 0), axis=1, keepdims=True), (16, 16))
        for l in range(blocks)
    ]
    count = jnp.zeros((16, 16), jnp.int32)
    found = [jnp.full((16, 16), blocks * 16, jnp.int32) for _ in range(blocks)]
    for k in range(blocks):
        for l in range(blocks):
            hit = left[k] == right[l]
            for s in range(min(blocks, k + 1)):
                found[s] = jnp.where(jnp.logical_and(hit, count == s), k * 16 + l, found[s])
            count = count + hit.astype(jnp.int32)
    table[...] = jnp.zeros_like(table)
    more[...] = jnp.zeros_like(more)
    for s in range(blocks):
        table[s, :, 0:16] = found[s]
    for s in range(SLOTS, blocks):
        more[s - SLOTS, :, 0:16] = found[s]
    count = jnp.where(at_col == row, 0, count)
    more[blocks - SLOTS, :, 0:16] = count
    more[blocks - SLOTS + 1, 0:1, 0:16] = jnp.max(count, axis=0, keepdims=True)
    fill = pltpu.make_async_copy(table, slots, local_sem.at[3])
    fill.start()
    fill.wait()
    for n, (a, b) in enumerate(zip(col_order(), row_order())):
        col_at[n] = a
        row_at[n] = b

    kept = []

    def keep(src, dst):
        copy = pltpu.make_async_copy(src, dst, local_sem.at[4 + len(kept)])
        copy.start()
        kept.append(copy)

    def hold_col(n):
        slot = col_order()[n]
        src = own if n == 0 else cols.at[slot]
        keep(src, cols_hbm.at[slot])
        for k in range(blocks):
            held_cols[n * blocks + k] = src[k]

    def hold_row(n):
        slot = row_order()[n]
        src = scaled if n == 0 else rows.at[slot]
        keep(src, rows_hbm.at[slot])
        for k in range(blocks):
            held_rows[n * (blocks + 1) + k] = src[k]
        held_rows[n * (blocks + 1) + blocks] = jnp.zeros((seg, cells), jnp.bfloat16)

    def multiply(row_first, row_last, first, last, width=SLOTS):
        @pl.loop(first, last)
        def _(n):
            a = col_at[n]
            results = []
            for m in range(row_first, row_last):
                b = row_at[m]
                codes = [slots[s, a, b] for s in range(width)]
                lhs = jnp.concatenate([held_rows[m * (blocks + 1) + (c >> 4)] for c in codes], axis=1)
                rhs = jnp.concatenate([held_cols[n * blocks + (c & 15)] for c in codes], axis=1)
                results.append(lax.dot_general(lhs, rhs, NT, preferred_element_type=jnp.float32))
            for m, result in zip(range(row_first, row_last), results):
                total[n, m, :, 0:seg] = result

    def take_far(step):
        for d in (1, -1):
            taken("far", "b", d, step)

    def hold_cols(*which):
        for n in which:
            hold_col(n)

    hold_row(0)
    hold_col(0)
    keep(more, more_hbm)
    take_z("b", 1)
    take_y(0)
    take_z("a", 1)
    taken("side")
    slot = period(1 - x_lo, y, core)
    for d in (1, -1):
        send(("y", 1, d), rows.at[slot], rows.at[slot], y_dev[d])
    twin(1, 0, slot, 0, blocks)
    hold_cols(1, 2)
    take_z("b", 2)
    taken("far", "a", 1, 0)
    for d in (1, -1):
        send_z("p", d, 1)
    take_z("a", 2)
    take_y2(0)
    hold_cols(4, 5)
    taken("far", "b", 1, 0)
    hold_cols(3)
    for n in (1, 2, 3):
        hold_row(n)
    take_z("p", 1)
    take_twin(0)
    for n in range(4, 8):
        hold_row(n)
    multiply(0, 8, 0, 1, blocks)
    multiply(0, 8, 1, 3)
    take_z("b", 3)
    multiply(0, 8, 3, 6)
    take_y(1)
    take_z("a", 3)
    take_far(1)
    hold_cols(6, 7)
    multiply(0, 8, 6, 8)
    take_z("p", 2)
    take_y2(1)
    hold_cols(8, 9)
    multiply(0, 8, 8, 10)
    take_z("b", 4)
    take_far(2)
    hold_cols(10, 11)
    multiply(0, 8, 10, 12)
    take_twin(1)
    for n in range(8, 16):
        hold_row(n)
    multiply(8, 16, 0, 1, blocks)
    multiply(8, 16, 1, 4)
    take_z("a", 4)
    multiply(8, 16, 4, 8)
    take_z("p", 3)
    multiply(8, 16, 8, 12)
    hold_cols(12)
    multiply(0, 16, 12, 13)
    take_far(3)
    hold_cols(13, 14)
    multiply(0, 16, 13, 15)
    take_z("p", 4)
    take_far(4)
    hold_cols(15)
    multiply(0, 16, 15, 16)

    for copy in copies.values():
        copy.wait_send()
    for copy in kept:
        copy.wait()


def gather(ids, sens, cov):
    blocks, seg, cells = sens.shape
    shard = (16, blocks, seg, cells)
    copies = 64
    vmem = pl.BlockSpec(memory_space=pltpu.VMEM)
    hbm = pl.BlockSpec(memory_space=pl.ANY)
    return pl.pallas_call(
        gather_kernel,
        out_shape=(
            pltpu.VMEM((16, 16, seg, 128), jnp.float32),
            pltpu.HBM(shard, sens.dtype),
            pltpu.HBM(shard, sens.dtype),
            pltpu.HBM((blocks - SLOTS + 2, 16, 128), jnp.int32),
        ),
        in_specs=[hbm, hbm, hbm],
        out_specs=(vmem, hbm, hbm, hbm),
        scratch_shapes=[
            pltpu.VMEM(ids.shape, ids.dtype),
            pltpu.VMEM(cov.shape, cov.dtype),
            pltpu.VMEM(shard, sens.dtype),
            pltpu.VMEM(shard, sens.dtype),
            pltpu.VMEM((16 * blocks, seg, cells), sens.dtype),
            pltpu.VMEM((16 * (blocks + 1), seg, cells), sens.dtype),
            pltpu.VMEM((blocks, seg, cells), sens.dtype),
            pltpu.VMEM((blocks, seg, cells), sens.dtype),
            pltpu.VMEM((blocks, 16, 128), jnp.int32),
            pltpu.VMEM((blocks - SLOTS + 2, 16, 128), jnp.int32),
            pltpu.SMEM((blocks, 16, 128), jnp.int32),
            pltpu.SMEM((16,), jnp.int32),
            pltpu.SMEM((16,), jnp.int32),
            pltpu.SemaphoreType.DMA((4 + 33,)),
            pltpu.SemaphoreType.DMA((copies,)),
            pltpu.SemaphoreType.DMA((copies,)),
        ],
        compiler_params=pltpu.CompilerParams(collective_id=1, has_side_effects=True, vmem_limit_bytes=40 * 2**20),
        name="gather",
    )(ids, sens, cov)


def product_kernel(
    total, more_hbm, cols_hbm, rows_hbm, out_hbm,
    stage, more, row_of, col_of, entry, first_of, left, right, more_sem, left_sem, right_sem, out_sem,
):
    blocks, seg = cols_hbm.shape[1:3]
    tiles = 12
    fetch = pltpu.make_async_copy(more_hbm, more, more_sem.at[0])
    fetch.start()
    for n, (a, b) in enumerate(zip(col_order(), row_order())):
        col_of[a] = n
        row_of[b] = n
    lane = lax.broadcasted_iota(jnp.int32, (seg, 128), 1)

    def join(b):
        m = row_of[b]
        for q in range(4):
            part = [total[col_of[q * 4 + p], m] for p in range(4)]
            r1, r2, r3 = [pltpu.roll(part[p], 128 - 32 * p, axis=1) for p in (1, 2, 3)]
            joined = [
                jnp.where(lane < 96, part[0], r1),
                jnp.where(lane < 64, r1, r2),
                jnp.where(lane < 32, r2, r3),
            ]
            for t in range(3):
                stage[pl.ds(b * seg * tiles + q * 3 + t, seg, stride=tiles), :] = joined[t]

    def write(b):
        chunk = seg * tiles
        part = pl.ds(pl.multiple_of(b * chunk, chunk), chunk)
        return pltpu.make_async_copy(stage.at[part], out_hbm.at[part], out_sem.at[b])

    def late(b):
        return more[blocks - SLOTS + 1, 0, b] > SLOTS

    def scan_row(b, n):
        first_of[b] = n

        def scan(a, n):
            def put(s, n):
                entry[n] = (b * 16 + a) * 256 + more[s, a, b]
                return n + 1

            return lax.fori_loop(0, jnp.maximum(more[blocks - SLOTS, a, b] - SLOTS, 0), put, n)

        return lax.fori_loop(0, jnp.where(late(b), 16, 0), scan, n)

    def blocks_of(e):
        code = entry[e]
        i = e % BATCH
        a, b, k, l = (code >> 8) & 15, code >> 12, (code >> 4) & 15, code & 15
        return (
            a,
            pltpu.make_async_copy(rows_hbm.at[b, k], left.at[i], left_sem.at[i]),
            pltpu.make_async_copy(cols_hbm.at[a, l], right.at[i], right_sem.at[i]),
        )

    def start(e):
        _, lhs, rhs = blocks_of(e)
        lhs.start()
        rhs.start()

    def add(b):
        @pl.loop(first_of[b], first_of[b + 1])
        def _(e):
            @pl.when(e >= BATCH)
            def _():
                start(e)

            a, lhs, rhs = blocks_of(e)
            lhs.wait()
            rhs.wait()
            i = e % BATCH
            r = lax.dot_general(left[i], right[i], NT, preferred_element_type=jnp.float32)
            r = jnp.concatenate([r, jnp.zeros((seg, 128 - seg), jnp.float32)], axis=1)
            t = a * seg // 128
            shift = a * seg % 128
            r = pltpu.roll(r, shift, axis=1)
            base = b * seg * tiles
            here = pl.ds(base + t, seg, stride=tiles)
            stage[here, :] = stage[here, :] + jnp.where(lane >= shift, r, 0.0)
            there = pl.ds(base + jnp.minimum(t + 1, tiles - 1), seg, stride=tiles)
            stage[there, :] = stage[there, :] + jnp.where(lane < shift, r, 0.0)

    pl.loop(0, 4)(join)
    fetch.wait()
    n_more = lax.fori_loop(0, 16, scan_row, 0)
    first_of[16] = n_more
    pl.loop(0, jnp.minimum(n_more, BATCH))(start)

    @pl.loop(0, 4)
    def _(b):
        @pl.when(jnp.logical_not(late(b)))
        def _():
            write(b).start()

    @pl.loop(4, 10)
    def _(b):
        join(b)

        @pl.when(jnp.logical_not(late(b)))
        def _():
            write(b).start()

    @pl.loop(0, 16)
    def _(b):
        @pl.when(late(b))
        def _():
            @pl.when(b >= 10)
            def _():
                join(b)

            add(b)
            write(b).start()

    @pl.loop(10, 16)
    def _(b):
        @pl.when(jnp.logical_not(late(b)))
        def _():
            join(b)
            write(b).start()

    @pl.loop(0, 16)
    def _(b):
        write(b).wait()


def product(total, more, cols, rows):
    stations, blocks, seg, cells = cols.shape
    lines = stations * seg * stations * seg // 128
    hbm = pl.BlockSpec(memory_space=pl.ANY)
    return pl.pallas_call(
        product_kernel,
        out_shape=jax.ShapeDtypeStruct((lines, 128), jnp.float32),
        in_specs=[pl.BlockSpec(memory_space=pltpu.VMEM), hbm, hbm, hbm],
        out_specs=hbm,
        scratch_shapes=[
            pltpu.VMEM((lines, 128), jnp.float32),
            pltpu.SMEM(more.shape, jnp.int32),
            pltpu.SMEM((16,), jnp.int32),
            pltpu.SMEM((16,), jnp.int32),
            pltpu.SMEM((stations * stations * blocks,), jnp.int32),
            pltpu.SMEM((stations + 1,), jnp.int32),
            pltpu.VMEM((BATCH, seg, cells), cols.dtype),
            pltpu.VMEM((BATCH, seg, cells), cols.dtype),
            pltpu.SemaphoreType.DMA((1,)),
            pltpu.SemaphoreType.DMA((BATCH,)),
            pltpu.SemaphoreType.DMA((BATCH,)),
            pltpu.SemaphoreType.DMA((16,)),
        ],
        compiler_params=pltpu.CompilerParams(vmem_limit_bytes=14 * 2**20),
        name="product",
    )(total, more, cols, rows)


def body(sensitivity, block_ids, covariance):
    def in_hbm(x):
        return pltpu.with_memory_space_constraint(x, pltpu.HBM)

    ids = jnp.transpose(block_ids, (0, 2, 1))
    total, cols, rows, more = gather(in_hbm(ids), in_hbm(sensitivity[0, 0]), in_hbm(covariance))
    total = pltpu.with_memory_space_constraint(total, pltpu.VMEM)
    more, cols, rows = in_hbm(more), in_hbm(cols), in_hbm(rows)
    lines = product(total, more, cols, rows)
    stations, _, seg, _ = cols.shape
    return lines.reshape(1, stations * seg, 1, stations * seg)


def solution(mesh):
    placed = (P("row", "col", None, None, None), P(), P())
    return jax.shard_map(
        body, mesh=mesh, in_specs=placed, out_specs=P("row", None, "col", None), check_vma=False
    )
```

```python
import functools

import jax
import jax.numpy as jnp
from jax import lax
from jax.experimental import pallas as pl
from jax.experimental.pallas import tpu as pltpu
from jax.sharding import PartitionSpec as P

MESH = pl.DeviceIdType.MESH
NT = (((1,), (1,)), ((), ()))
NY, NZ = 4, 8
SLOTS = 4
BATCH = 16


def place():
    row = lax.axis_index("row")
    col = lax.axis_index("col")
    return row, col, row // 2, row % 2, col // 8, (col // 2) % 4, col % 2


def station(z, x_hi):
    return ((z + NZ) % NZ) * 2 + x_hi


def period(x_lo, y, core):
    return (x_lo * NY + (y + NY) % NY) * 2 + core


def row_order():
    _, _, _, _, x_lo, y, core = place()
    return [period(x, y + d, c) for x in (x_lo, 1 - x_lo) for c in (core, 1 - core) for d in (0, -1, 1, 2)]


def col_order():
    _, _, z, x_hi, _, _, _ = place()
    far = 1 - x_hi
    steps = [(0, x_hi), (-1, x_hi), (1, x_hi), (0, far), (-2, x_hi), (2, x_hi), (-1, far), (1, far)]
    steps += [(-3, x_hi), (3, x_hi), (-2, far), (2, far), (4, x_hi), (-3, far), (3, far), (4, far)]
    return [station(z + d, x) for d, x in steps]


def gather_kernel(
    ids_hbm, sens_ref, cov_hbm, total, cols_hbm, rows_hbm, more_hbm,
    ids_ref, cov_ref, cols, rows, held_cols, held_rows, own, scaled, table, more, slots, col_at, row_at, local_sem, send_sem, recv_sem,
):
    row, col, z, x_hi, x_lo, y, core = place()
    blocks, seg, cells = sens_ref.shape
    half = blocks // 2

    z_dev = {d: (station(z + d, x_hi), col) for d in (1, -1)}
    y_dev = {d: (row, period(x_lo, y + d, core)) for d in (1, -1)}
    far_dev = (station(z, 1 - x_hi), col)
    side_dev = (row, period(1 - x_lo, y, core))
    twin_dev = (row, period(x_lo, y, 1 - core))

    barrier = pltpu.get_barrier_semaphore()
    partners = [z_dev[1], z_dev[-1], y_dev[1], y_dev[-1], far_dev, side_dev, twin_dev]
    for device in partners:
        pl.semaphore_signal(barrier, inc=1, device_id=device, device_id_type=MESH)
    loads = [
        pltpu.make_async_copy(src, dst, local_sem.at[n])
        for n, (src, dst) in enumerate([(sens_ref, own), (ids_hbm, ids_ref), (cov_hbm, cov_ref)])
    ]
    for load in loads:
        load.start()
    pl.semaphore_wait(barrier, len(partners))

    copies = {}

    def send(key, src, dst, device):
        n = len(copies)
        copy = pltpu.make_async_remote_copy(
            src_ref=src, dst_ref=dst, send_sem=send_sem.at[n], recv_sem=recv_sem.at[n], device_id=device, device_id_type=MESH
        )
        copy.start()
        copies[key] = copy

    def taken(*key):
        copies[key].wait_recv()

    def piece(kind, d, step):
        first = half if kind == "b" else 0
        if step < 4:
            return pl.ds(first, half), pl.ds(0, seg)
        return pl.ds(first, half), pl.ds(0 if d == 1 else seg // 2, seg // 2)

    def send_z(kind, d, step):
        part = piece(kind, d, step)
        slot = station(z - d * (step - 1), 1 - x_hi if kind == "p" else x_hi)
        src = sens_ref if (step == 1 and kind != "p") else cols.at[slot]
        send(("z", kind, d, step), src.at[part], cols.at[(slot, *part)], z_dev[d])

    def send_far(kind, d, step):
        part = piece(kind, d, step)
        slot = station(z - d * step, x_hi)
        src = sens_ref if step == 0 else cols.at[slot]
        send(("far", kind, d, step), src.at[part], cols.at[(slot, *part)], far_dev)

    def take_z(kind, step):
        for d in (1, -1):
            taken("z", kind, d, step)
            if step < 4:
                send_z(kind, d, step + 1)
            if kind == "b":
                send_far(kind, d, step)

    for kind in "ba":
        for d in (1, -1):
            send_z(kind, d, 1)

    for load in loads:
        load.wait()
    lane = lax.broadcasted_iota(jnp.int32, (1, 16), 1)
    model = lax.broadcasted_iota(jnp.int32, (cov_ref.shape[0], 1), 0)
    for k in range(blocks):
        mine = jnp.sum(jnp.where(lane == col, ids_ref[row, k : k + 1, :], 0), axis=1, keepdims=True)
        factor = jnp.sum(jnp.where(model == mine, cov_ref[...], 0.0), axis=0, keepdims=True)
        scaled[k] = (own[k].astype(jnp.float32) * factor).astype(jnp.bfloat16)
    send(("side",), scaled, rows.at[col], side_dev)
    for d in (1, -1):
        send(("y", 0, d), scaled, rows.at[col], y_dev[d])
    send(("twin", 0, 0), scaled, rows.at[col], twin_dev)
    send_far("a", 1, 0)
    send_far("b", 1, 0)

    def twin(line, shift, slot, first, size):
        ref = rows.at[slot, pl.ds(first, size)]
        send(("twin", line, shift), ref, ref, twin_dev)

    def take_y(line):
        for d in (1, -1):
            taken("y", line, d)
            slot = period(x_lo if line == 0 else 1 - x_lo, y - d, core)
            ref = rows.at[slot, pl.ds(0 if d == 1 else half, half)]
            send(("y2", line, d), ref, ref, y_dev[d])
            twin(line, d, slot, 0, blocks)

    def take_y2(line):
        for d in (1, -1):
            taken("y2", line, d)
            slot = period(x_lo if line == 0 else 1 - x_lo, y - 2 * d, core)
            twin(line, 2 * d, slot, 0 if d == 1 else half, half)

    def take_twin(line):
        for shift in (0, 1, -1, 2, -2):
            taken("twin", line, shift)

    at_col = lax.broadcasted_iota(jnp.int32, (16, 16), 0)
    at_row = lax.broadcasted_iota(jnp.int32, (16, 16), 1)
    left = [jnp.broadcast_to(ids_ref[row, k : k + 1, :], (16, 16)) for k in range(blocks)]
    right = [
        jnp.broadcast_to(jnp.sum(jnp.where(at_row == col, ids_ref[:, l, :], 0), axis=1, keepdims=True), (16, 16))
        for l in range(blocks)
    ]
    count = jnp.zeros((16, 16), jnp.int32)
    found = [jnp.full((16, 16), blocks * 16, jnp.int32) for _ in range(blocks)]
    for k in range(blocks):
        for l in range(blocks):
            hit = left[k] == right[l]
            for s in range(min(blocks, k + 1)):
                found[s] = jnp.where(jnp.logical_and(hit, count == s), k * 16 + l, found[s])
            count = count + hit.astype(jnp.int32)
    table[...] = jnp.zeros_like(table)
    more[...] = jnp.zeros_like(more)
    for s in range(blocks):
        table[s, :, 0:16] = found[s]
    for s in range(SLOTS, blocks):
        more[s - SLOTS, :, 0:16] = found[s]
    count = jnp.where(at_col == row, 0, count)
    more[blocks - SLOTS, :, 0:16] = count
    more[blocks - SLOTS + 1, 0:1, 0:16] = jnp.max(count, axis=0, keepdims=True)
    fill = pltpu.make_async_copy(table, slots, local_sem.at[3])
    fill.start()
    fill.wait()
    for n, (a, b) in enumerate(zip(col_order(), row_order())):
        col_at[n] = a
        row_at[n] = b

    kept = []

    def keep(src, dst):
        copy = pltpu.make_async_copy(src, dst, local_sem.at[4 + len(kept)])
        copy.start()
        kept.append(copy)

    def hold_col(n):
        slot = col_order()[n]
        src = own if n == 0 else cols.at[slot]
        keep(src, cols_hbm.at[slot])
        for k in range(blocks):
            held_cols[n * blocks + k] = src[k]

    def hold_row(n):
        slot = row_order()[n]
        src = scaled if n == 0 else rows.at[slot]
        keep(src, rows_hbm.at[slot])
        for k in range(blocks):
            held_rows[n * (blocks + 1) + k] = src[k]
        held_rows[n * (blocks + 1) + blocks] = jnp.zeros((seg, cells), jnp.bfloat16)

    def multiply(row_first, row_last, first, last, width=SLOTS):
        @pl.loop(first, last)
        def _(n):
            a = col_at[n]
            results = []
            for m in range(row_first, row_last):
                b = row_at[m]
                codes = [slots[s, a, b] for s in range(width)]
                lhs = jnp.concatenate([held_rows[m * (blocks + 1) + (c >> 4)] for c in codes], axis=1)
                rhs = jnp.concatenate([held_cols[n * blocks + (c & 15)] for c in codes], axis=1)
                results.append(lax.dot_general(lhs, rhs, NT, preferred_element_type=jnp.float32))
            for m, result in zip(range(row_first, row_last), results):
                total[n, m, :, 0:seg] = result

    def take_far(step):
        for d in (1, -1):
            taken("far", "b", d, step)

    def hold_cols(*which):
        for n in which:
            hold_col(n)

    hold_row(0)
    hold_col(0)
    keep(more, more_hbm)
    take_z("b", 1)
    take_y(0)
    take_z("a", 1)
    taken("side")
    slot = period(1 - x_lo, y, core)
    for d in (1, -1):
        send(("y", 1, d), rows.at[slot], rows.at[slot], y_dev[d])
    twin(1, 0, slot, 0, blocks)
    hold_cols(1, 2)
    take_z("b", 2)
    taken("far", "a", 1, 0)
    for d in (1, -1):
        send_z("p", d, 1)
    take_z("a", 2)
    take_y2(0)
    hold_cols(4, 5)
    taken("far", "b", 1, 0)
    hold_cols(3)
    for n in (1, 2, 3):
        hold_row(n)
    take_z("p", 1)
    take_twin(0)
    for n in range(4, 8):
        hold_row(n)
    multiply(0, 8, 0, 1, blocks)
    multiply(0, 8, 1, 3)
    take_z("b", 3)
    multiply(0, 8, 3, 6)
    take_y(1)
    take_z("a", 3)
    take_far(1)
    hold_cols(6, 7)
    multiply(0, 8, 6, 8)
    take_z("p", 2)
    take_y2(1)
    hold_cols(8, 9)
    multiply(0, 8, 8, 10)
    take_z("b", 4)
    take_far(2)
    hold_cols(10, 11)
    multiply(0, 8, 10, 12)
    take_twin(1)
    for n in range(8, 16):
        hold_row(n)
    multiply(8, 16, 0, 1, blocks)
    multiply(8, 16, 1, 4)
    take_z("a", 4)
    multiply(8, 16, 4, 8)
    take_z("p", 3)
    multiply(8, 16, 8, 12)
    hold_cols(12)
    multiply(0, 16, 12, 13)
    take_far(3)
    hold_cols(13, 14)
    multiply(0, 16, 13, 15)
    take_z("p", 4)
    take_far(4)
    hold_cols(15)
    multiply(0, 16, 15, 16)

    for copy in copies.values():
        copy.wait_send()
    for copy in kept:
        copy.wait()


def gather(ids, sens, cov):
    blocks, seg, cells = sens.shape
    shard = (16, blocks, seg, cells)
    copies = 64
    vmem = pl.BlockSpec(memory_space=pltpu.VMEM)
    hbm = pl.BlockSpec(memory_space=pl.ANY)
    return pl.pallas_call(
        gather_kernel,
        out_shape=(
            pltpu.VMEM((16, 16, seg, 128), jnp.float32),
            pltpu.HBM(shard, sens.dtype),
            pltpu.HBM(shard, sens.dtype),
            pltpu.HBM((blocks - SLOTS + 2, 16, 128), jnp.int32),
        ),
        in_specs=[hbm, hbm, hbm],
        out_specs=(vmem, hbm, hbm, hbm),
        scratch_shapes=[
            pltpu.VMEM(ids.shape, ids.dtype),
            pltpu.VMEM(cov.shape, cov.dtype),
            pltpu.VMEM(shard, sens.dtype),
            pltpu.VMEM(shard, sens.dtype),
            pltpu.VMEM((16 * blocks, seg, cells), sens.dtype),
            pltpu.VMEM((16 * (blocks + 1), seg, cells), sens.dtype),
            pltpu.VMEM((blocks, seg, cells), sens.dtype),
            pltpu.VMEM((blocks, seg, cells), sens.dtype),
            pltpu.VMEM((blocks, 16, 128), jnp.int32),
            pltpu.VMEM((blocks - SLOTS + 2, 16, 128), jnp.int32),
            pltpu.SMEM((blocks, 16, 128), jnp.int32),
            pltpu.SMEM((16,), jnp.int32),
            pltpu.SMEM((16,), jnp.int32),
            pltpu.SemaphoreType.DMA((4 + 33,)),
            pltpu.SemaphoreType.DMA((copies,)),
            pltpu.SemaphoreType.DMA((copies,)),
        ],
        compiler_params=pltpu.CompilerParams(collective_id=1, has_side_effects=True, vmem_limit_bytes=40 * 2**20),
        name="gather",
    )(ids, sens, cov)


def product_kernel(
    total, more_hbm, cols_hbm, rows_hbm, out_hbm,
    stage, more, row_of, col_of, entry, first_of, left, right, more_sem, left_sem, right_sem, out_sem,
):
    blocks, seg = cols_hbm.shape[1:3]
    tiles = 12
    fetch = pltpu.make_async_copy(more_hbm, more, more_sem.at[0])
    fetch.start()
    for n, (a, b) in enumerate(zip(col_order(), row_order())):
        col_of[a] = n
        row_of[b] = n
    lane = lax.broadcasted_iota(jnp.int32, (seg, 128), 1)

    def join(b):
        m = row_of[b]
        for q in range(4):
            part = [total[col_of[q * 4 + p], m] for p in range(4)]
            r1, r2, r3 = [pltpu.roll(part[p], 128 - 32 * p, axis=1) for p in (1, 2, 3)]
            joined = [
                jnp.where(lane < 96, part[0], r1),
                jnp.where(lane < 64, r1, r2),
                jnp.where(lane < 32, r2, r3),
            ]
            for t in range(3):
                stage[pl.ds(b * seg * tiles + q * 3 + t, seg, stride=tiles), :] = joined[t]

    def write(b):
        chunk = seg * tiles
        part = pl.ds(pl.multiple_of(b * chunk, chunk), chunk)
        return pltpu.make_async_copy(stage.at[part], out_hbm.at[part], out_sem.at[b])

    def late(b):
        return more[blocks - SLOTS + 1, 0, b] > SLOTS

    def scan_row(b, n):
        first_of[b] = n

        def scan(a, n):
            def put(s, n):
                entry[n] = (b * 16 + a) * 256 + more[s, a, b]
                return n + 1

            return lax.fori_loop(0, jnp.maximum(more[blocks - SLOTS, a, b] - SLOTS, 0), put, n)

        return lax.fori_loop(0, jnp.where(late(b), 16, 0), scan, n)

    def blocks_of(e):
        code = entry[e]
        i = e % BATCH
        a, b, k, l = (code >> 8) & 15, code >> 12, (code >> 4) & 15, code & 15
        return (
            a,
            pltpu.make_async_copy(rows_hbm.at[b, k], left.at[i], left_sem.at[i]),
            pltpu.make_async_copy(cols_hbm.at[a, l], right.at[i], right_sem.at[i]),
        )

    def start(e):
        _, lhs, rhs = blocks_of(e)
        lhs.start()
        rhs.start()

    def add(b):
        @pl.loop(first_of[b], first_of[b + 1])
        def _(e):
            @pl.when(e >= BATCH)
            def _():
                start(e)

            a, lhs, rhs = blocks_of(e)
            lhs.wait()
            rhs.wait()
            i = e % BATCH
            r = lax.dot_general(left[i], right[i], NT, preferred_element_type=jnp.float32)
            r = jnp.concatenate([r, jnp.zeros((seg, 128 - seg), jnp.float32)], axis=1)
            t = a * seg // 128
            shift = a * seg % 128
            r = pltpu.roll(r, shift, axis=1)
            base = b * seg * tiles
            here = pl.ds(base + t, seg, stride=tiles)
            stage[here, :] = stage[here, :] + jnp.where(lane >= shift, r, 0.0)
            there = pl.ds(base + jnp.minimum(t + 1, tiles - 1), seg, stride=tiles)
            stage[there, :] = stage[there, :] + jnp.where(lane < shift, r, 0.0)

    @pl.loop(0, 4)
    def _(b):
        join(b)
        write(b).start()

    fetch.wait()
    n_more = lax.fori_loop(0, 16, scan_row, 0)
    first_of[16] = n_more
    pl.loop(0, jnp.minimum(n_more, BATCH))(start)

    @pl.loop(4, 10)
    def _(b):
        join(b)

        @pl.when(jnp.logical_not(late(b)))
        def _():
            write(b).start()

    @pl.loop(0, 16)
    def _(b):
        @pl.when(late(b))
        def _():
            @pl.when(b < 4)
            def _():
                write(b).wait()

            @pl.when(b >= 10)
            def _():
                join(b)

            add(b)
            write(b).start()

    @pl.loop(10, 16)
    def _(b):
        @pl.when(jnp.logical_not(late(b)))
        def _():
            join(b)
            write(b).start()

    @pl.loop(0, 16)
    def _(b):
        write(b).wait()


def product(total, more, cols, rows):
    stations, blocks, seg, cells = cols.shape
    lines = stations * seg * stations * seg // 128
    hbm = pl.BlockSpec(memory_space=pl.ANY)
    return pl.pallas_call(
        product_kernel,
        out_shape=jax.ShapeDtypeStruct((lines, 128), jnp.float32),
        in_specs=[pl.BlockSpec(memory_space=pltpu.VMEM), hbm, hbm, hbm],
        out_specs=hbm,
        scratch_shapes=[
            pltpu.VMEM((lines, 128), jnp.float32),
            pltpu.SMEM(more.shape, jnp.int32),
            pltpu.SMEM((16,), jnp.int32),
            pltpu.SMEM((16,), jnp.int32),
            pltpu.SMEM((stations * stations * blocks,), jnp.int32),
            pltpu.SMEM((stations + 1,), jnp.int32),
            pltpu.VMEM((BATCH, seg, cells), cols.dtype),
            pltpu.VMEM((BATCH, seg, cells), cols.dtype),
            pltpu.SemaphoreType.DMA((1,)),
            pltpu.SemaphoreType.DMA((BATCH,)),
            pltpu.SemaphoreType.DMA((BATCH,)),
            pltpu.SemaphoreType.DMA((16,)),
        ],
        compiler_params=pltpu.CompilerParams(vmem_limit_bytes=14 * 2**20),
        name="product",
    )(total, more, cols, rows)


def body(sensitivity, block_ids, covariance):
    def in_hbm(x):
        return pltpu.with_memory_space_constraint(x, pltpu.HBM)

    ids = jnp.transpose(block_ids, (0, 2, 1))
    total, cols, rows, more = gather(in_hbm(ids), in_hbm(sensitivity[0, 0]), in_hbm(covariance))
    total = pltpu.with_memory_space_constraint(total, pltpu.VMEM)
    more, cols, rows = in_hbm(more), in_hbm(cols), in_hbm(rows)
    lines = product(total, more, cols, rows)
    stations, _, seg, _ = cols.shape
    return lines.reshape(1, stations * seg, 1, stations * seg)


def solution(mesh):
    placed = (P("row", "col", None, None, None), P(), P())
    return jax.shard_map(
        body, mesh=mesh, in_specs=placed, out_specs=P("row", None, "col", None), check_vma=False
    )
```
